32 devices in a mesh: groups: 2 (over y), graph: 8 (over z, x), dp: 2 (over core).
Axes of the slice: x: 2, y: 2, z: 4, core: 2. Of those that a mesh axis runs over, the one named last changes fastest.
Arguments:
- embed: bfloat16 [2, 64, 12544], P('dp', ('groups', 'graph')), parts along dimension 1, may hold values from -6 to 6
- cotangent: bfloat16 [2, 64, 12544], P('dp', ('groups', 'graph')), parts along dimension 1, may hold values from -6 to 6
- rotation: bfloat16 [2, 49, 49, 1024], P('dp', None, None, ('groups', 'graph')), parts along dimension 3, as said below
- distance_feat: bfloat16 [2, 1024, 512], P('dp', ('groups', 'graph')), parts along dimension 1, may hold values from 0 to 1
- src_owner: int32 [2, 1024, 1], P('dp', ('groups', 'graph')), parts along dimension 1, may hold values from 0 to 7; in each aligned block of 64 rows (0 to 63, 64 to 127, ..., all dimensions but the last counted through in order) at most 16 rows name the same one
- src_local: int32 [2, 1024], P('dp', ('groups', 'graph')), parts along dimension 1, may hold values from 0 to 3
- tgt_local: int32 [2, 1024], P('dp', ('groups', 'graph')), parts along dimension 1, may hold values from 0 to 3
- live_count: int32 [2, 16], P('dp', ('groups', 'graph')), parts along dimension 1, may hold values from 16 to 64
- w_src: bfloat16 [256, 256], replicated, may hold values from -0.375 to 0.375
- w_tgt: bfloat16 [256, 256], replicated, may hold values from -0.375 to 0.375
- w_radial: bfloat16 [512, 256], replicated, may hold values from -0.25 to 0.25
Outputs:
- grad_embed: bfloat16 [2, 64, 12544], P('dp', ('groups', 'graph')), parts along dimension 1
- grad_w_src: float32 [512, 256], P('groups'), parts along dimension 0
- grad_w_tgt: float32 [512, 256], P('groups'), parts along dimension 0
- grad_w_radial: float32 [1024, 256], P('groups'), parts along dimension 0
The draws below stay inside these ranges and needn't reach their ends.
There are 2 independent parts, one for each index of `groups`. The reference program is written for one: setup_inputs(seed, part) draws one part's arguments, and reference() takes and returns one part's arrays. A program takes and returns all parts, laid end to end along the dimension named above; an argument that names none is the same for every part. Nothing has to cross between parts.
Inputs may be any that keep to these rules, and one draw needn't show every extreme that they name: `src_owner`: among the 64 edge slots of one device, at most 16 have their source on any one device; this most is reached. The live slots of a device's block are its first live_count ones. `rotation`: block diagonal: entries coupling different degrees are zero.
All inputs are finite; a program needn't handle non-finite values.
Results may differ from the reference program's by a relative error of at most 0.0085.
Values may be sent and summed in bfloat16 or wider, within the bound.
A program may use at most 64 MiB of HBM per device.

```python
import math
import jax
import jax.numpy as jnp
import numpy as np
from jax import lax

LMAX = 6
COEFFS = 49
WIDTH = 256
RADIAL = 512
E_DEV = 64
A_DEV = 4
CAP = 16
EDGES = 512
ATOMS = 32
BATCHES = 2
N_GRAPH = 8


def draw_rotation(key, part):
    key = jax.random.fold_in(key, 5)
    index = jnp.arange(COEFFS)
    squares = jnp.arange(1, LMAX + 1) ** 2
    degree = jnp.sum((index[:, None] >= squares[None, :]).astype(jnp.int32), axis=1)
    same_degree = degree[:, None] == degree[None, :]
    spread = 0.6 / jnp.sqrt((2 * degree + 1).astype(jnp.float32))
    noise = jax.random.normal(key, (BATCHES, COEFFS, COEFFS, EDGES), jnp.float32) * spread[None, :, None, None]
    identity = jnp.eye(COEFFS, dtype=jnp.float32)
    result = jnp.where(same_degree[None, :, :, None], noise, 0.0) + 0.8 * identity[None, :, :, None]
    return result.astype(jnp.bfloat16)


def plant(array, own_key, smallest, high):
    longest = array.shape.index(max(array.shape))
    spots = []
    for shift in (0, 1):
        where = [jax.random.randint(jax.random.fold_in(own_key, axis), (), 0, length) for axis, length in enumerate(array.shape)]
        where[longest] = (where[longest] + shift) % array.shape[longest]
        spots.append(tuple(where))
    return array.at[spots[0]].set(smallest).at[spots[1]].set(high)


def block_levels(rng, shape, cuts, least, top_value):
    level, own = 1.0, jax.random.fold_in(rng, 6)
    for dim, parts in cuts:
        draws = jnp.exp(jax.random.uniform(jax.random.fold_in(own, dim), (parts,), jnp.float32, least / len(cuts), top_value / len(cuts)))
        level = level * jnp.repeat(draws, shape[dim] // parts).reshape([-1 if axis == dim else 1 for axis in range(len(shape))])
    return level


def assign_block(key, own, number, rows, amount, top, bound, lean):
    order = jax.random.permutation(key, amount)
    packed, usual = shares(amount, rows * top, bound, lean, True), shares(amount, rows * top, bound, lean, False)
    places = jnp.arange(amount)

    def named(sizes, turn):
        used = int((sizes > 0).sum())
        fixed = max(1, used // 4)
        shifted = fixed + (places - fixed + turn * (used - fixed)) % max(1, amount - fixed)
        return jnp.zeros((amount,), jnp.int32).at[order[jnp.where(places < fixed, places, shifted)]].set(jnp.asarray(sizes, jnp.int32))

    sizes = jnp.where(number % 4 == 0, named(packed, number // 4), named(usual, number - number // 4 - 1))
    mixed = jax.random.permutation(jax.random.fold_in(own, 3), amount)
    donor, sink = mixed[0:amount // 2 * 2:2], mixed[1:amount // 2 * 2:2]
    margin = jnp.minimum(sizes[donor] - 1, bound - sizes[sink]) // 2
    margin = jnp.where((donor == order[0]) | (sink == order[0]) | (sizes[sink] == 0), 0, jnp.maximum(margin, 0))
    shifted = jax.random.randint(jax.random.fold_in(own, 4), (amount // 2,), 0, 1 << 20) % (margin + 1)
    sizes = sizes.at[donor].add(-shifted).at[sink].add(shifted)
    members = jnp.searchsorted(jnp.cumsum(sizes), jnp.arange(rows * top), side="right").astype(jnp.int32)
    listing = members.reshape(top, rows).T
    listing = listing[jax.random.permutation(jax.random.fold_in(own, 1), rows)]
    turn = jax.random.randint(jax.random.fold_in(own, 2), (rows, 1), 0, top)
    return jnp.take_along_axis(listing, (jnp.arange(top)[None, :] + turn) % top, axis=1)


def shares(count, total, reach, skew, full):
    weights = [(1 << 20) // math.isqrt(rank ** skew) + 1 for rank in range(1, count + 1)]
    largest = reach if full else min(reach, max(-(-total // count), total * weights[0] // sum(weights)))
    least = 1 if total - largest >= count - 1 else 0
    counts, rest = [largest] + [least] * (count - 1), total - largest - least * (count - 1)
    while rest > 0:
        free = [i for i in range(1, count) if counts[i] < largest] or [i for i in range(1, count) if counts[i] < reach]
        pool, left = sum([weights[i] for i in free]), rest
        for i in free:
            extra = min(reach - counts[i], max(1, left * weights[i] // pool), rest)
            counts[i] = counts[i] + extra
            rest = rest - extra
    return np.array(counts)


def centred(key, shape, scale, limit, pieces=(), held_as=jnp.bfloat16):
    factor_of = block_levels(key, shape, pieces, -0.22, 0.18) if pieces else 1.0
    values = jax.random.normal(key, shape, jnp.float32) * scale * factor_of
    return jnp.minimum(jnp.maximum(values, -limit), limit).astype(held_as)


def setup_inputs(seed: int = 0, part: int = 0) -> dict:
    key_of = jax.random.split(jax.random.key(seed), 12)
    own_keys = jax.random.split(jax.random.fold_in(key_of[11], part), 12)
    embed = centred(own_keys[0], (BATCHES, ATOMS, COEFFS * WIDTH), 1.0, 6.0, ((0, 2), (1, 8)))
    cotangent = centred(own_keys[1], (BATCHES, ATOMS, COEFFS * WIDTH), 1.0, 6.0, ((0, 2), (1, 8)))
    rotation = draw_rotation(jax.random.fold_in(jax.random.fold_in(key_of[11], part), 71), part)
    distance_feat = jnp.clip(1.0 * jax.random.uniform(own_keys[3], (BATCHES, EDGES, RADIAL), jnp.float32) ** block_levels(own_keys[3], (BATCHES, EDGES, RADIAL), ((0, 2), (1, 8)), -0.2, 0.2), 0.0, 1.0).astype(jnp.bfloat16)
    src_owner_keys = jax.random.split(jax.random.fold_in(own_keys[4], 1), BATCHES * EDGES // E_DEV)
    src_owner_turns = jax.random.permutation(jax.random.fold_in(own_keys[4], 3), BATCHES * EDGES // E_DEV)
    src_owner = jax.vmap(lambda own, number: assign_block(jax.random.fold_in(own_keys[4], 2), own, number, E_DEV, N_GRAPH, 1, CAP, 2))(src_owner_keys, src_owner_turns).reshape((BATCHES, EDGES, 1))
    src_local = plant(jax.random.randint(own_keys[5], (BATCHES, EDGES), 0, A_DEV), jax.random.fold_in(own_keys[5], 1), 0, A_DEV - 1).astype(jnp.int32)
    tgt_local = plant(jax.random.randint(own_keys[6], (BATCHES, EDGES), 0, A_DEV), jax.random.fold_in(own_keys[6], 1), 0, A_DEV - 1).astype(jnp.int32)
    live_count = plant(jax.random.randint(own_keys[7], (BATCHES, N_GRAPH), E_DEV // 4, E_DEV + 1), jax.random.fold_in(own_keys[7], 1), E_DEV // 4, E_DEV).astype(jnp.int32)
    w_src = centred(key_of[8], (WIDTH, WIDTH), WIDTH ** -0.5, 0.375)
    w_tgt = centred(key_of[9], (WIDTH, WIDTH), WIDTH ** -0.5, 0.375)
    w_radial = centred(key_of[10], (RADIAL, WIDTH), RADIAL ** -0.5, 0.25)
    return {"embed": embed, "cotangent": cotangent, "rotation": rotation, "distance_feat": distance_feat, "src_owner": src_owner, "src_local": src_local, "tgt_local": tgt_local, "live_count": live_count, "w_src": w_src, "w_tgt": w_tgt, "w_radial": w_radial}


def reference(embed, cotangent, rotation, distance_feat, src_owner, src_local, tgt_local, live_count, w_src, w_tgt, w_radial):
    highest = lax.Precision.HIGHEST
    block_size = math.gcd(EDGES, 512)
    row_len = COEFFS * WIDTH
    acc_src = jnp.zeros((WIDTH, WIDTH), jnp.float32)
    acc_tgt = jnp.zeros((WIDTH, WIDTH), jnp.float32)
    acc_rad = jnp.zeros((RADIAL, WIDTH), jnp.float32)
    outputs = []
    for batch_idx in range(BATCHES):
        slot_ids = jnp.arange(EDGES, dtype=jnp.int32)
        source_ids = (src_owner[batch_idx, :, 0] * A_DEV + src_local[batch_idx]).astype(jnp.int32)
        target_ids = (slot_ids // E_DEV * A_DEV + tgt_local[batch_idx]).astype(jnp.int32)
        is_live = slot_ids % E_DEV < live_count[batch_idx][slot_ids // E_DEV]
        emb_rows = embed[batch_idx]
        cot_rows = cotangent[batch_idx]
        rot_all = rotation[batch_idx]
        dist_all = distance_feat[batch_idx]

        def advance(carry, block_index):
            grad_rows, sum_src, sum_tgt, sum_rad = carry
            first = (block_index * block_size).astype(jnp.int32)
            ids_src = lax.dynamic_slice_in_dim(source_ids, first, block_size)
            ids_tgt = lax.dynamic_slice_in_dim(target_ids, first, block_size)
            live_blk = lax.dynamic_slice_in_dim(is_live, first, block_size)
            rot_blk = lax.dynamic_slice_in_dim(rot_all, first, block_size, 2).astype(jnp.float32)
            dist_blk = lax.dynamic_slice_in_dim(dist_all, first, block_size, 0)
            src_blk = emb_rows[ids_src].reshape(block_size, COEFFS, WIDTH).astype(jnp.float32)
            tgt_blk = emb_rows[ids_tgt].reshape(block_size, COEFFS, WIDTH).astype(jnp.float32)
            cot_blk = jnp.where(live_blk[:, None], cot_rows[ids_tgt], jnp.zeros((), jnp.bfloat16))
            cot_blk = cot_blk.reshape(block_size, COEFFS, WIDTH).astype(jnp.float32)
            rot_src = jnp.einsum('ije,ejc->eic', rot_blk, src_blk, precision=highest).astype(jnp.bfloat16)
            rot_tgt = jnp.einsum('ije,ejc->eic', rot_blk, tgt_blk, precision=highest).astype(jnp.bfloat16)
            flat_src = rot_src.reshape(-1, WIDTH)
            flat_tgt = rot_tgt.reshape(-1, WIDTH)
            conv_out = jnp.dot(flat_src, w_src, preferred_element_type=jnp.float32) + jnp.dot(flat_tgt, w_tgt, preferred_element_type=jnp.float32)
            radial_pre = jnp.dot(dist_blk, w_radial, preferred_element_type=jnp.float32)
            sigmoid_val = jax.nn.sigmoid(radial_pre)
            gate = radial_pre * sigmoid_val
            rot_cot = jnp.einsum('ije,ejc->eic', rot_blk, cot_blk, precision=highest).astype(jnp.bfloat16)
            gate_grad = lax.optimization_barrier(jnp.sum(rot_cot.astype(jnp.float32) * conv_out.reshape(block_size, COEFFS, WIDTH), axis=1))
            conv_grad = (gate[:, None, :] * rot_cot.astype(jnp.float32)).astype(jnp.bfloat16)
            flat_grad = conv_grad.reshape(-1, WIDTH)
            pre_grad = (gate_grad * (sigmoid_val + radial_pre * sigmoid_val * (1.0 - sigmoid_val))).astype(jnp.bfloat16)
            sum_src = sum_src + jnp.dot(flat_src.T, flat_grad, preferred_element_type=jnp.float32)
            sum_tgt = sum_tgt + jnp.dot(flat_tgt.T, flat_grad, preferred_element_type=jnp.float32)
            sum_rad = sum_rad + jnp.dot(dist_blk.T, pre_grad, preferred_element_type=jnp.float32)
            back_src = jnp.dot(flat_grad, w_src.T, preferred_element_type=jnp.float32).astype(jnp.bfloat16)
            back_tgt = jnp.dot(flat_grad, w_tgt.T, preferred_element_type=jnp.float32).astype(jnp.bfloat16)
            back_src = back_src.reshape(block_size, COEFFS, WIDTH).astype(jnp.float32)
            back_tgt = back_tgt.reshape(block_size, COEFFS, WIDTH).astype(jnp.float32)
            send_src = jnp.einsum('jie,ejc->eic', rot_blk, back_src, precision=highest).astype(jnp.bfloat16)
            keep_tgt = jnp.einsum('jie,ejc->eic', rot_blk, back_tgt, precision=highest).astype(jnp.bfloat16)
            grad_rows = grad_rows.at[ids_src].add(send_src.reshape(block_size, row_len).astype(jnp.float32))
            grad_rows = grad_rows.at[ids_tgt].add(keep_tgt.reshape(block_size, row_len).astype(jnp.float32))
            return ((grad_rows, sum_src, sum_tgt, sum_rad), None)
        start_rows = jnp.zeros((ATOMS, row_len), jnp.float32)
        carry, unused = lax.scan(advance, (start_rows, acc_src, acc_tgt, acc_rad), jnp.arange(EDGES // block_size, dtype=jnp.int32))
        grad_rows, acc_src, acc_tgt, acc_rad = carry
        outputs.append(grad_rows.astype(jnp.bfloat16))
    scale = 1.0 / math.sqrt(BATCHES * EDGES * COEFFS)
    grad_embed = jnp.stack(outputs, axis=0)
    return (grad_embed, acc_src * scale, acc_tgt * scale, acc_rad * scale)
```

```python
import functools
import math

import jax
import jax.numpy as jnp
from jax import lax
from jax.experimental import pallas as pl
from jax.experimental.pallas import tpu as pltpu
from jax.sharding import PartitionSpec as P


def shards(
    embed,
    cotangent,
    rotation,
    distance_feat,
    src_owner,
    src_local,
    tgt_local,
    live_count,
    w_src,
    w_tgt,
    w_radial,
):
    peer_count = lax.axis_size("graph")
    atom_count = embed.shape[1]
    row_len = embed.shape[2]
    coeffs = rotation.shape[1]
    edge_count = rotation.shape[3]
    channels = w_src.shape[0]
    slot_count = max(2, 2 * edge_count // peer_count)
    block_size = math.gcd(edge_count, 32)
    owners = src_owner[0, :, 0]
    local_index = src_local[0]
    matches = (owners[:, None] == jnp.arange(peer_count, dtype=jnp.int32)[None, :]).astype(
        jnp.int32
    )
    before = jnp.cumsum(matches, axis=0) - matches
    slot_rank = jnp.sum(before * matches, axis=1)
    position = owners * slot_count + slot_rank
    placed = position[:, None] == jnp.arange(peer_count * slot_count, dtype=jnp.int32)[None, :]
    wanted = jnp.sum(jnp.where(placed, local_index[:, None], 0), axis=0).reshape(
        peer_count, slot_count
    )
    requested = lax.all_to_all(wanted, "graph", split_axis=0, concat_axis=0, tiled=True)
    own_rows = embed[0]
    outgoing = jnp.take(own_rows, requested.reshape(-1), axis=0).reshape(
        peer_count, slot_count, row_len
    )
    arrived = lax.all_to_all(outgoing, "graph", split_axis=0, concat_axis=0, tiled=True).reshape(
        peer_count * slot_count, row_len
    )
    source_rows = jnp.take(arrived, position, axis=0)
    target_ids = tgt_local[0]
    is_live = jnp.arange(edge_count, dtype=jnp.int32) < live_count[0, 0]
    target_rows = jnp.take(own_rows, target_ids, axis=0)
    cot_rows = jnp.where(
        is_live[:, None], jnp.take(cotangent[0], target_ids, axis=0), jnp.zeros((), jnp.bfloat16)
    )
    rot_all = rotation[0]
    dist_all = distance_feat[0]
    contract_rows = (((0,), (0,)), ((), ()))
    contract_cols = (((1,), (1,)), ((), ()))

    def edge_block(block_index, carry):
        sum_src, sum_tgt, sum_rad, outbound, target_sum = carry
        first = block_index * block_size
        rot_blk = lax.dynamic_slice_in_dim(rot_all, first, block_size, 2)
        src_blk = lax.dynamic_slice_in_dim(source_rows, first, block_size, 0).reshape(
            block_size, coeffs, channels
        )
        tgt_blk = lax.dynamic_slice_in_dim(target_rows, first, block_size, 0).reshape(
            block_size, coeffs, channels
        )
        cot_blk = lax.dynamic_slice_in_dim(cot_rows, first, block_size, 0).reshape(
            block_size, coeffs, channels
        )
        dist_blk = lax.dynamic_slice_in_dim(dist_all, first, block_size, 0)
        ids_blk = lax.dynamic_slice_in_dim(target_ids, first, block_size, 0)
        rot_src = jnp.einsum(
            "ije,ejc->eic", rot_blk, src_blk, preferred_element_type=jnp.float32
        ).astype(jnp.bfloat16)
        rot_tgt = jnp.einsum(
            "ije,ejc->eic", rot_blk, tgt_blk, preferred_element_type=jnp.float32
        ).astype(jnp.bfloat16)
        flat_src = rot_src.reshape(-1, channels)
        flat_tgt = rot_tgt.reshape(-1, channels)
        conv_out = jnp.dot(flat_src, w_src, preferred_element_type=jnp.float32) + jnp.dot(
            flat_tgt, w_tgt, preferred_element_type=jnp.float32
        )
        radial_pre = jnp.dot(dist_blk, w_radial, preferred_element_type=jnp.float32)
        sigmoid_val = jax.nn.sigmoid(radial_pre)
        gate = radial_pre * sigmoid_val
        rot_cot = jnp.einsum(
            "ije,ejc->eic", rot_blk, cot_blk, preferred_element_type=jnp.float32
        ).astype(jnp.bfloat16)
        gate_grad = jnp.sum(
            rot_cot.astype(jnp.float32) * conv_out.reshape(block_size, coeffs, channels), axis=1
        )
        conv_grad = (gate[:, None, :] * rot_cot).astype(jnp.bfloat16)
        flat_grad = conv_grad.reshape(-1, channels)
        pre_grad = (
            gate_grad * (sigmoid_val + radial_pre * sigmoid_val * (1.0 - sigmoid_val))
        ).astype(jnp.bfloat16)
        sum_src = sum_src + lax.dot_general(
            flat_src, flat_grad, contract_rows, preferred_element_type=jnp.float32
        )
        sum_tgt = sum_tgt + lax.dot_general(
            flat_tgt, flat_grad, contract_rows, preferred_element_type=jnp.float32
        )
        sum_rad = sum_rad + lax.dot_general(
            dist_blk, pre_grad, contract_rows, preferred_element_type=jnp.float32
        )
        back_src = lax.dot_general(
            flat_grad, w_src, contract_cols, preferred_element_type=jnp.float32
        ).astype(jnp.bfloat16)
        back_tgt = lax.dot_general(
            flat_grad, w_tgt, contract_cols, preferred_element_type=jnp.float32
        ).astype(jnp.bfloat16)
        back_src = back_src.reshape(block_size, coeffs, channels)
        back_tgt = back_tgt.reshape(block_size, coeffs, channels)
        send_src = jnp.einsum(
            "jie,ejc->eic", rot_blk, back_src, preferred_element_type=jnp.float32
        ).astype(jnp.bfloat16)
        keep_tgt = jnp.einsum(
            "jie,ejc->eic", rot_blk, back_tgt, preferred_element_type=jnp.float32
        ).astype(jnp.bfloat16)
        outbound = lax.dynamic_update_slice_in_dim(
            outbound, send_src.reshape(block_size, row_len), first, 0
        )
        target_hits = (jnp.arange(atom_count, dtype=jnp.int32)[:, None] == ids_blk[None, :]).astype(
            jnp.bfloat16
        )
        target_sum = target_sum + jnp.dot(
            target_hits, keep_tgt.reshape(block_size, row_len), preferred_element_type=jnp.float32
        )
        return (sum_src, sum_tgt, sum_rad, outbound, target_sum)

    initial = (
        jnp.zeros((channels, channels), jnp.float32),
        jnp.zeros((channels, channels), jnp.float32),
        jnp.zeros((w_radial.shape[0], channels), jnp.float32),
        jnp.zeros((edge_count, row_len), jnp.bfloat16),
        jnp.zeros((atom_count, row_len), jnp.float32),
    )
    block_total = edge_count // block_size
    sum_src, sum_tgt, sum_rad, outbound, target_sum = lax.fori_loop(
        0, block_total, edge_block, initial
    )
    bucket = jnp.zeros((peer_count * slot_count, row_len), jnp.bfloat16).at[position].set(outbound)
    returned = lax.all_to_all(
        bucket.reshape(peer_count, slot_count, row_len),
        "graph",
        split_axis=0,
        concat_axis=0,
        tiled=True,
    )
    returned = returned.reshape(peer_count * slot_count, row_len)
    owner_hits = (
        jnp.arange(atom_count, dtype=jnp.int32)[:, None] == requested.reshape(-1)[None, :]
    ).astype(jnp.bfloat16)
    source_sum = jnp.dot(owner_hits, returned, preferred_element_type=jnp.float32)
    grad_embed = (source_sum + target_sum).astype(jnp.bfloat16)[None]
    total_src, total_tgt, total_rad = lax.psum((sum_src, sum_tgt, sum_rad), ("graph", "dp"))
    scale = 1.0 / math.sqrt(lax.axis_size("dp") * edge_count * peer_count * coeffs)
    return (grad_embed, total_src * scale, total_tgt * scale, total_rad * scale)


def remote(src, dst, send_sem, recv_sem, device):
    return pltpu.make_async_remote_copy(
        src_ref=src,
        dst_ref=dst,
        send_sem=send_sem,
        recv_sem=recv_sem,
        device_id=device,
        device_id_type=pl.DeviceIdType.MESH,
    )


def dot(a, b, dims=(((1,), (0,)), ((), ()))):
    return lax.dot_general(a, b, dims, preferred_element_type=jnp.float32)


FIRST = (((0,), (0,)), ((), ()))
LAST = (((1,), (1,)), ((), ()))


def block_kernel(
    peers,
    scale,
    emb,
    cot,
    rot,
    dist,
    keys,
    tgt,
    live,
    w_src,
    w_tgt,
    w_rad,
    out_embed,
    out_src,
    out_tgt,
    out_rad,
    atoms,
    y_all,
    y_tgt,
    rot_rows,
    cot_rows,
    cot_half,
    held,
    gate,
    slope,
    pick,
    place,
    sums,
    kept,
    from_x,
    to_z,
    from_z,
    part_tgt,
    part_rad,
    part_src,
    core_tgt,
    core_rad,
    core_src,
    early,
    early_in,
    late,
    late_in,
    whole,
    y_send,
    y_recv,
    f_send,
    x_send,
    x_recv,
    z_send,
    z_recv,
    c_send,
    c_recv,
    e_send,
    e_recv,
    l_send,
    l_recv,
    g_send,
    g_recv,
    h_send,
    h_recv,
):
    coeffs, edges, width = rot.shape[0], rot.shape[2], w_src.shape[0]
    atom_count = emb.shape[0]
    groups = -(-coeffs // 4)
    tall = rot_rows.shape[0] // edges
    deep = cot_half.shape[1]
    columns = peers // 2
    parts = width // 128
    me, core = lax.axis_index("graph"), lax.axis_index("dp")
    z, x = lax.div(me, 2), lax.rem(me, 2)
    beside = {"graph": z * 2 + 1 - x}
    other = {"dp": 1 - core}
    started = []

    def send(*args):
        copy = remote(*args)
        copy.start()
        started.append(copy)

    def wide(ref, first, last):
        return jnp.concatenate([ref[part, first:last, :] for part in range(parts)], axis=1)

    def arrived(ref, sem):
        remote(ref, ref, sem, sem, other).wait_recv()

    barrier = pltpu.get_barrier_semaphore()
    for step in range(1, peers):
        pl.semaphore_signal(
            barrier,
            inc=1,
            device_id={"graph": lax.rem(me + step, peers)},
            device_id_type=pl.DeviceIdType.MESH,
        )
    pl.semaphore_signal(barrier, inc=1, device_id=other, device_id_type=pl.DeviceIdType.MESH)

    for group in range(groups):
        rows = []
        for c in range(4 * group, 4 * group + 4):
            if c < coeffs:
                rows.append(emb[:, c * width : (c + 1) * width].astype(jnp.float32))
            else:
                rows.append(jnp.zeros((atom_count, width), jnp.float32))
        atoms[16 * group : 16 * group + 16, :] = jnp.concatenate(rows, axis=0).astype(jnp.bfloat16)
    y_all[me] = dot(atoms[...], w_src[...]).astype(jnp.bfloat16)
    pl.semaphore_wait(barrier, peers)
    for step in range(1, columns):
        to = {"graph": lax.rem(z + step, columns) * 2 + x}
        send(y_all.at[me], y_all.at[me], y_send.at[step], y_recv.at[me], to)
    send(y_all.at[me], y_all.at[me], y_send.at[0], y_recv.at[me], beside)
    y_tgt[...] = dot(atoms[...], w_tgt[...]).astype(jnp.bfloat16)

    pre = dot(dist[...], w_rad[...])
    sig = jax.nn.sigmoid(pre)
    alive = lax.broadcasted_iota(jnp.int32, (edges, width), 0) < live[0, 0]
    gate[...] = jnp.where(alive, pre * sig, 0.0)
    slope[...] = jnp.where(alive, sig + pre * sig * (1.0 - sig), 0.0)

    row = lax.broadcasted_iota(jnp.int32, (256, 256), 0)
    k, a = lax.rem(lax.div(row, 4), 4), lax.rem(row, 4)
    src_rows = 16 * peers
    key_src = jnp.broadcast_to(keys[0:1, :], (256, 256))
    key_tgt = jnp.broadcast_to(keys[1:2, :], (256, 256))
    hit_src = (k * (4 * peers) + lax.div(row, 16) * 4 + a) == key_src
    hit_tgt = (k * 4 + a) == key_tgt
    hit = ((row < src_rows) & hit_src) | ((row >= src_rows) & (row < src_rows + 16) & hit_tgt)
    ones = jnp.where(hit, 1.0, 0.0)
    pick[...] = ones.astype(jnp.bfloat16)
    place[...] = ones.T.astype(jnp.bfloat16)

    rot_rows[...] = jnp.zeros_like(rot_rows)
    cot_rows[...] = jnp.zeros_like(cot_rows)
    for c in range(coeffs):
        block = rot[c].astype(jnp.float32)
        block = jnp.concatenate([block, jnp.zeros((deep - coeffs, edges), jnp.float32)], axis=0)
        rot_rows[c * edges : (c + 1) * edges, 0:deep] = block.T
        line = cot[:, c * width : (c + 1) * width].astype(jnp.float32)
        for part in range(parts):
            cot_rows[part, pl.ds(c, atom_count, stride=deep), :] = line[:, part * 128 : part * 128 + 128]
    cot_half[...] = wide(cot_rows, 0, atom_count * deep).reshape(cot_half.shape).astype(jnp.bfloat16)

    def edge(e, unused):
        r = rot_rows[pl.ds(e, tall, stride=edges), :][:, 0:deep].astype(jnp.bfloat16)
        turned = dot(r, cot_half[tgt[0, e]]).astype(jnp.bfloat16)
        back = dot(r, turned, FIRST)[0:tall]
        for part in range(parts):
            held[part, pl.ds(e, tall, stride=edges), :] = back[:, part * 128 : part * 128 + 128]
        return unused

    def forward(step):
        block = lax.rem(z - step + columns, columns) * 2 + x
        arrived(y_all.at[block], y_recv.at[block])
        send(y_all.at[block], y_all.at[block], f_send.at[step], y_recv.at[block], beside)

    for part in range(4):
        lax.fori_loop(part * (edges // 4), (part + 1) * (edges // 4), edge, 0, unroll=8)
        if 1 <= part < columns:
            forward(part)
    for step in range(4, columns):
        forward(step)

    for group in range(groups):
        rows = slice(group * 4 * edges, (group + 1) * 4 * edges)
        gated = wide(held, rows.start, rows.stop).reshape(4, edges, width) * gate[...][None]
        total = dot(pick[...], gated.reshape(4 * edges, width).astype(jnp.bfloat16))
        for p in range(peers):
            sums[p, 16 * group : 16 * group + 16, :] = total[16 * p : 16 * p + 16].astype(
                jnp.bfloat16
            )
        kept[16 * group : 16 * group + 16, :] = total[src_rows : src_rows + 16].astype(jnp.bfloat16)
    for step in list(range(1, columns)) + [0]:
        goal = lax.rem(z + step, columns)
        send(sums.at[goal * 2 + 1 - x], from_x.at[goal], x_send.at[step], x_recv.at[goal], beside)

    half = width // 2
    part_tgt[...] = (
        dot(atoms[...], kept[...], FIRST).astype(jnp.bfloat16).reshape(part_tgt.shape)
    )
    send(part_tgt.at[1 - core], core_tgt, c_send.at[0], c_recv.at[0], other)

    for step in range(columns):
        block = step * 2 + 1 - x
        arrived(y_all.at[block], y_recv.at[block])
    gate_grad = jnp.zeros((edges, width), jnp.float32)
    spare = jnp.zeros((256 - src_rows - 16, width), jnp.bfloat16)
    for group in range(groups):
        near = [y_all[p, 16 * group : 16 * group + 16, :] for p in range(peers)]
        near = jnp.concatenate(near + [y_tgt[16 * group : 16 * group + 16, :], spare], axis=0)
        mixed = dot(place[...], near) * wide(
            held, group * 4 * edges, (group + 1) * 4 * edges
        )
        gate_grad = gate_grad + jnp.sum(mixed.reshape(4, edges, width), axis=0)
    pre_grad = (gate_grad * slope[...]).astype(jnp.bfloat16)
    part_rad[...] = dot(dist[...], pre_grad, FIRST).astype(jnp.bfloat16).reshape(part_rad.shape)
    send(part_rad.at[1 - core], core_rad, c_send.at[1], c_recv.at[1], other)

    for step in range(1, columns):
        goal = lax.rem(z + step, columns)
        arrived(from_x.at[goal], x_recv.at[goal])
        to_z[goal] = (
            sums[goal * 2 + x].astype(jnp.float32) + from_x[goal].astype(jnp.float32)
        ).astype(jnp.bfloat16)
        send(to_z.at[goal], from_z.at[z], z_send.at[step], z_recv.at[z], {"graph": goal * 2 + x})

    arrived(core_tgt, c_recv.at[0])
    arrived(core_rad, c_recv.at[1])
    cut_tgt, cut_rad = half // peers, w_rad.shape[0] // 2 // peers
    both_tgt = part_tgt[core].astype(jnp.float32) + core_tgt[...].astype(jnp.float32)
    both_rad = part_rad[core].astype(jnp.float32) + core_rad[...].astype(jnp.float32)
    early[:, 0:cut_tgt, :] = both_tgt.reshape(peers, cut_tgt, width).astype(jnp.bfloat16)
    early[:, cut_tgt:, :] = both_rad.reshape(peers, cut_rad, width).astype(jnp.bfloat16)
    for step in range(1, peers):
        p = lax.rem(me + step, peers)
        send(early.at[p], early_in.at[me], e_send.at[step], e_recv.at[me], {"graph": p})

    arrived(from_x.at[z], x_recv.at[z])
    total = sums[me].astype(jnp.float32) + from_x[z].astype(jnp.float32)
    for step in range(1, columns):
        origin = lax.rem(z + step, columns)
        arrived(from_z.at[origin], z_recv.at[origin])
        total = total + from_z[origin].astype(jnp.float32)
    total = total.astype(jnp.bfloat16)
    part_src[...] = dot(atoms[...], total, FIRST).astype(jnp.bfloat16).reshape(part_src.shape)
    send(part_src.at[1 - core], core_src, c_send.at[2], c_recv.at[2], other)
    back = dot(total, w_src[...], LAST) + dot(kept[...], w_tgt[...], LAST)
    for c in range(coeffs):
        out_embed[:, c * width : (c + 1) * width] = back[4 * c : 4 * c + 4].astype(jnp.bfloat16)
    arrived(core_src, c_recv.at[2])
    both_src = part_src[core].astype(jnp.float32) + core_src[...].astype(jnp.float32)
    late[...] = both_src.reshape(late.shape).astype(jnp.bfloat16)
    for step in range(1, peers):
        p = lax.rem(me + step, peers)
        send(late.at[p], late_in.at[me], l_send.at[step], l_recv.at[me], {"graph": p})

    first = early[me].astype(jnp.float32)
    second = late[me].astype(jnp.float32)
    for step in range(1, peers):
        p = lax.rem(me + step, peers)
        arrived(early_in.at[p], e_recv.at[p])
        first = first + early_in[p].astype(jnp.float32)
    for step in range(1, peers):
        p = lax.rem(me + step, peers)
        arrived(late_in.at[p], l_recv.at[p])
        second = second + late_in[p].astype(jnp.float32)
    split = cut_tgt + cut_rad
    whole[core, me, 0:split, :] = first.astype(jnp.bfloat16)
    whole[core, me, split:, :] = second.astype(jnp.bfloat16)
    mine = whole.at[core, me]
    for step in range(1, peers):
        p = lax.rem(me + step, peers)
        send(mine, mine, g_send.at[step], g_recv.at[me], {"graph": p})
    send(mine, mine, h_send.at[0], h_recv.at[me], other)

    def spread(c, p):
        piece = whole[c, p].astype(jnp.float32) * scale
        at_tgt = pl.ds(pl.multiple_of(c * half + p * cut_tgt, cut_tgt), cut_tgt)
        at_rad = pl.ds(pl.multiple_of((c * peers + p) * cut_rad, cut_rad), cut_rad)
        out_tgt[at_tgt, :] = piece[0:cut_tgt]
        out_rad[at_rad, :] = piece[cut_tgt:split]
        out_src[at_tgt, :] = piece[split:]

    spread(core, me)
    for step in range(1, peers):
        p = lax.rem(me + step, peers)
        arrived(whole.at[core, p], g_recv.at[p])
        send(whole.at[core, p], whole.at[core, p], h_send.at[step], h_recv.at[p], other)
        spread(core, p)
    for step in range(peers):
        p = lax.rem(me + step, peers)
        arrived(whole.at[1 - core, p], h_recv.at[p])
        spread(1 - core, p)
    for copy in started:
        copy.wait_send()


def near_shards(
    embed,
    cotangent,
    rotation,
    distance_feat,
    src_owner,
    src_local,
    tgt_local,
    live_count,
    w_src,
    w_tgt,
    w_radial,
):
    peers = lax.axis_size("graph")
    columns = peers // 2
    atom_count, row_len = embed.shape[1:]
    coeffs, edges = rotation.shape[1], rotation.shape[3]
    width, radial = w_src.shape[0], w_radial.shape[0]
    groups = -(-coeffs // 4)
    tall = -(-groups * 4 // 8) * 8
    deep = -(-tall // 16) * 16
    scale = 1.0 / math.sqrt(lax.axis_size("dp") * edges * peers * coeffs)
    lane = jnp.arange(4, dtype=jnp.int32)[:, None]
    key_src = lane * (4 * peers) + (src_owner[0, :, 0] * atom_count + src_local[0])[None, :]
    key_tgt = lane * 4 + tgt_local[0][None, :]
    keys = jnp.stack([key_src.reshape(-1), key_tgt.reshape(-1)])
    half, cut = width // 2, width // 2 // peers
    rows = 16 * groups
    bf16, f32 = jnp.bfloat16, jnp.float32
    split = cut + radial // 2 // peers
    vmem = pl.BlockSpec(memory_space=pltpu.VMEM)
    smem = pl.BlockSpec(memory_space=pltpu.SMEM)
    dma = pltpu.SemaphoreType.DMA
    scratch = [
        pltpu.VMEM((rows, width), bf16),
        pltpu.VMEM((peers, rows, width), bf16),
        pltpu.VMEM((rows, width), bf16),
        pltpu.VMEM((tall * edges, 128), f32),
        pltpu.VMEM((width // 128, atom_count * deep, 128), f32),
        pltpu.VMEM((atom_count, deep, width), bf16),
        pltpu.VMEM((width // 128, tall * edges, 128), f32),
        pltpu.VMEM((edges, width), f32),
        pltpu.VMEM((edges, width), f32),
        pltpu.VMEM((256, 256), bf16),
        pltpu.VMEM((256, 256), bf16),
        pltpu.VMEM((peers, rows, width), bf16),
        pltpu.VMEM((rows, width), bf16),
        pltpu.VMEM((columns, rows, width), bf16),
        pltpu.VMEM((columns, rows, width), bf16),
        pltpu.VMEM((columns, rows, width), bf16),
        pltpu.VMEM((2, half, width), bf16),
        pltpu.VMEM((2, radial // 2, width), bf16),
        pltpu.VMEM((2, half, width), bf16),
        pltpu.VMEM((half, width), bf16),
        pltpu.VMEM((radial // 2, width), bf16),
        pltpu.VMEM((half, width), bf16),
        pltpu.VMEM((peers, split, width), bf16),
        pltpu.VMEM((peers, split, width), bf16),
        pltpu.VMEM((peers, cut, width), bf16),
        pltpu.VMEM((peers, cut, width), bf16),
        pltpu.VMEM((2, peers, split + cut, width), bf16),
    ]
    counts = [peers, peers, columns, columns, columns, columns, columns, 3, 3] + [peers] * 8
    grad_embed, grad_src, grad_tgt, grad_rad = pl.pallas_call(
        functools.partial(block_kernel, peers, scale),
        out_shape=(
            jax.ShapeDtypeStruct((atom_count, row_len), bf16),
            jax.ShapeDtypeStruct((width, width), f32),
            jax.ShapeDtypeStruct((width, width), f32),
            jax.ShapeDtypeStruct((radial, width), f32),
        ),
        in_specs=[vmem] * 5 + [smem] * 2 + [vmem] * 3,
        out_specs=(vmem,) * 4,
        scratch_shapes=scratch + [dma((count,)) for count in counts],
        compiler_params=pltpu.CompilerParams(
            collective_id=0, has_side_effects=True, vmem_limit_bytes=40 * 1024 * 1024
        ),
    )(
        embed[0],
        cotangent[0],
        rotation[0],
        distance_feat[0],
        keys,
        tgt_local,
        live_count,
        w_src,
        w_tgt,
        w_radial,
    )
    return grad_embed[None], grad_src, grad_tgt, grad_rad


def solution(mesh):
    peers = mesh.shape["graph"]
    near = peers in (4, 8) and mesh.shape["dp"] == 2
    placed = (
        P("dp", ("groups", "graph"), None),
        P("dp", ("groups", "graph"), None),
        P("dp", None, None, ("groups", "graph")),
        P("dp", ("groups", "graph"), None),
        P("dp", ("groups", "graph"), None),
        P("dp", ("groups", "graph")),
        P("dp", ("groups", "graph")),
        P("dp", ("groups", "graph")),
        P(),
        P(),
        P(),
    )
    return jax.shard_map(
        near_shards if near else shards,
        mesh=mesh,
        in_specs=placed,
        out_specs=(
            P("dp", ("groups", "graph"), None),
            P("groups", None),
            P("groups", None),
            P("groups", None),
        ),
        check_vma=False,
    )
```

```python
import functools
import math

import jax
import jax.numpy as jnp
from jax import lax
from jax.experimental import pallas as pl
from jax.experimental.pallas import tpu as pltpu
from jax.sharding import PartitionSpec as P


def shards(
    embed,
    cotangent,
    rotation,
    distance_feat,
    src_owner,
    src_local,
    tgt_local,
    live_count,
    w_src,
    w_tgt,
    w_radial,
):
    peer_count = lax.axis_size("graph")
    atom_count = embed.shape[1]
    row_len = embed.shape[2]
    coeffs = rotation.shape[1]
    edge_count = rotation.shape[3]
    channels = w_src.shape[0]
    slot_count = max(2, 2 * edge_count // peer_count)
    block_size = math.gcd(edge_count, 32)
    owners = src_owner[0, :, 0]
    local_index = src_local[0]
    matches = (owners[:, None] == jnp.arange(peer_count, dtype=jnp.int32)[None, :]).astype(
        jnp.int32
    )
    before = jnp.cumsum(matches, axis=0) - matches
    slot_rank = jnp.sum(before * matches, axis=1)
    position = owners * slot_count + slot_rank
    placed = position[:, None] == jnp.arange(peer_count * slot_count, dtype=jnp.int32)[None, :]
    wanted = jnp.sum(jnp.where(placed, local_index[:, None], 0), axis=0).reshape(
        peer_count, slot_count
    )
    requested = lax.all_to_all(wanted, "graph", split_axis=0, concat_axis=0, tiled=True)
    own_rows = embed[0]
    outgoing = jnp.take(own_rows, requested.reshape(-1), axis=0).reshape(
        peer_count, slot_count, row_len
    )
    arrived = lax.all_to_all(outgoing, "graph", split_axis=0, concat_axis=0, tiled=True).reshape(
        peer_count * slot_count, row_len
    )
    source_rows = jnp.take(arrived, position, axis=0)
    target_ids = tgt_local[0]
    is_live = jnp.arange(edge_count, dtype=jnp.int32) < live_count[0, 0]
    target_rows = jnp.take(own_rows, target_ids, axis=0)
    cot_rows = jnp.where(
        is_live[:, None], jnp.take(cotangent[0], target_ids, axis=0), jnp.zeros((), jnp.bfloat16)
    )
    rot_all = rotation[0]
    dist_all = distance_feat[0]
    contract_rows = (((0,), (0,)), ((), ()))
    contract_cols = (((1,), (1,)), ((), ()))

    def edge_block(block_index, carry):
        sum_src, sum_tgt, sum_rad, outbound, target_sum = carry
        first = block_index * block_size
        rot_blk = lax.dynamic_slice_in_dim(rot_all, first, block_size, 2)
        src_blk = lax.dynamic_slice_in_dim(source_rows, first, block_size, 0).reshape(
            block_size, coeffs, channels
        )
        tgt_blk = lax.dynamic_slice_in_dim(target_rows, first, block_size, 0).reshape(
            block_size, coeffs, channels
        )
        cot_blk = lax.dynamic_slice_in_dim(cot_rows, first, block_size, 0).reshape(
            block_size, coeffs, channels
        )
        dist_blk = lax.dynamic_slice_in_dim(dist_all, first, block_size, 0)
        ids_blk = lax.dynamic_slice_in_dim(target_ids, first, block_size, 0)
        rot_src = jnp.einsum(
            "ije,ejc->eic", rot_blk, src_blk, preferred_element_type=jnp.float32
        ).astype(jnp.bfloat16)
        rot_tgt = jnp.einsum(
            "ije,ejc->eic", rot_blk, tgt_blk, preferred_element_type=jnp.float32
        ).astype(jnp.bfloat16)
        flat_src = rot_src.reshape(-1, channels)
        flat_tgt = rot_tgt.reshape(-1, channels)
        conv_out = jnp.dot(flat_src, w_src, preferred_element_type=jnp.float32) + jnp.dot(
            flat_tgt, w_tgt, preferred_element_type=jnp.float32
        )
        radial_pre = jnp.dot(dist_blk, w_radial, preferred_element_type=jnp.float32)
        sigmoid_val = jax.nn.sigmoid(radial_pre)
        gate = radial_pre * sigmoid_val
        rot_cot = jnp.einsum(
            "ije,ejc->eic", rot_blk, cot_blk, preferred_element_type=jnp.float32
        ).astype(jnp.bfloat16)
        gate_grad = jnp.sum(
            rot_cot.astype(jnp.float32) * conv_out.reshape(block_size, coeffs, channels), axis=1
        )
        conv_grad = (gate[:, None, :] * rot_cot).astype(jnp.bfloat16)
        flat_grad = conv_grad.reshape(-1, channels)
        pre_grad = (
            gate_grad * (sigmoid_val + radial_pre * sigmoid_val * (1.0 - sigmoid_val))
        ).astype(jnp.bfloat16)
        sum_src = sum_src + lax.dot_general(
            flat_src, flat_grad, contract_rows, preferred_element_type=jnp.float32
        )
        sum_tgt = sum_tgt + lax.dot_general(
            flat_tgt, flat_grad, contract_rows, preferred_element_type=jnp.float32
        )
        sum_rad = sum_rad + lax.dot_general(
            dist_blk, pre_grad, contract_rows, preferred_element_type=jnp.float32
        )
        back_src = lax.dot_general(
            flat_grad, w_src, contract_cols, preferred_element_type=jnp.float32
        ).astype(jnp.bfloat16)
        back_tgt = lax.dot_general(
            flat_grad, w_tgt, contract_cols, preferred_element_type=jnp.float32
        ).astype(jnp.bfloat16)
        back_src = back_src.reshape(block_size, coeffs, channels)
        back_tgt = back_tgt.reshape(block_size, coeffs, channels)
        send_src = jnp.einsum(
            "jie,ejc->eic", rot_blk, back_src, preferred_element_type=jnp.float32
        ).astype(jnp.bfloat16)
        keep_tgt = jnp.einsum(
            "jie,ejc->eic", rot_blk, back_tgt, preferred_element_type=jnp.float32
        ).astype(jnp.bfloat16)
        outbound = lax.dynamic_update_slice_in_dim(
            outbound, send_src.reshape(block_size, row_len), first, 0
        )
        target_hits = (jnp.arange(atom_count, dtype=jnp.int32)[:, None] == ids_blk[None, :]).astype(
            jnp.bfloat16
        )
        target_sum = target_sum + jnp.dot(
            target_hits, keep_tgt.reshape(block_size, row_len), preferred_element_type=jnp.float32
        )
        return (sum_src, sum_tgt, sum_rad, outbound, target_sum)

    initial = (
        jnp.zeros((channels, channels), jnp.float32),
        jnp.zeros((channels, channels), jnp.float32),
        jnp.zeros((w_radial.shape[0], channels), jnp.float32),
        jnp.zeros((edge_count, row_len), jnp.bfloat16),
        jnp.zeros((atom_count, row_len), jnp.float32),
    )
    block_total = edge_count // block_size
    sum_src, sum_tgt, sum_rad, outbound, target_sum = lax.fori_loop(
        0, block_total, edge_block, initial
    )
    bucket = jnp.zeros((peer_count * slot_count, row_len), jnp.bfloat16).at[position].set(outbound)
    returned = lax.all_to_all(
        bucket.reshape(peer_count, slot_count, row_len),
        "graph",
        split_axis=0,
        concat_axis=0,
        tiled=True,
    )
    returned = returned.reshape(peer_count * slot_count, row_len)
    owner_hits = (
        jnp.arange(atom_count, dtype=jnp.int32)[:, None] == requested.reshape(-1)[None, :]
    ).astype(jnp.bfloat16)
    source_sum = jnp.dot(owner_hits, returned, preferred_element_type=jnp.float32)
    grad_embed = (source_sum + target_sum).astype(jnp.bfloat16)[None]
    total_src, total_tgt, total_rad = lax.psum((sum_src, sum_tgt, sum_rad), ("graph", "dp"))
    scale = 1.0 / math.sqrt(lax.axis_size("dp") * edge_count * peer_count * coeffs)
    return (grad_embed, total_src * scale, total_tgt * scale, total_rad * scale)


def remote(src, dst, send_sem, recv_sem, device):
    return pltpu.make_async_remote_copy(
        src_ref=src,
        dst_ref=dst,
        send_sem=send_sem,
        recv_sem=recv_sem,
        device_id=device,
        device_id_type=pl.DeviceIdType.MESH,
    )


def dot(a, b, dims=(((1,), (0,)), ((), ()))):
    return lax.dot_general(a, b, dims, preferred_element_type=jnp.float32)


FIRST = (((0,), (0,)), ((), ()))
LAST = (((1,), (1,)), ((), ()))


def block_kernel(
    peers,
    scale,
    emb_hbm,
    cot_hbm,
    rot_hbm,
    dist_hbm,
    owner_hbm,
    local_hbm,
    tgt_hbm,
    live_hbm,
    w_src_hbm,
    w_tgt_hbm,
    w_rad_hbm,
    out_embed,
    out_src,
    out_tgt,
    out_rad,
    emb,
    cot,
    rot,
    dist,
    owner,
    local,
    near_tgt,
    tgt,
    live,
    w_src,
    w_tgt,
    w_rad,
    x_all,
    y_all,
    y_tgt,
    rot_rows,
    cot_rows,
    cot_half,
    held,
    gate,
    slope,
    pick,
    place,
    sums,
    kept,
    from_x,
    to_z,
    from_z,
    share,
    core_in,
    both,
    both_x,
    both_z,
    both_in,
    whole,
    load,
    y_send,
    y_recv,
    f_send,
    x_send,
    x_recv,
    z_send,
    z_recv,
    c_send,
    c_recv,
    d_send,
    d_recv,
    e_send,
    e_recv,
    g_send,
    g_recv,
    h_send,
    h_recv,
):
    coeffs, edges, width = rot.shape[0], rot.shape[2], w_src.shape[0]
    atom_count = emb.shape[0]
    groups = -(-coeffs // 4)
    tall = rot_rows.shape[0] // edges
    deep = cot_half.shape[1]
    columns = peers // 2
    parts = width // 128
    me, core = lax.axis_index("graph"), lax.axis_index("dp")
    z, x = lax.div(me, 2), lax.rem(me, 2)
    beside = {"graph": z * 2 + 1 - x}
    other = {"dp": 1 - core}
    started = []
    loads = {}
    pairs = (
        ("emb", emb_hbm, emb),
        ("w_rad", w_rad_hbm, w_rad),
        ("dist", dist_hbm, dist),
        ("live", live_hbm, live),
        ("tgt", tgt_hbm, tgt),
        ("rot", rot_hbm, rot),
        ("cot", cot_hbm, cot),
        ("owner", owner_hbm, owner),
        ("local", local_hbm, local),
        ("near_tgt", tgt_hbm, near_tgt),
        ("w_src", w_src_hbm, w_src),
        ("w_tgt", w_tgt_hbm, w_tgt),
    )
    for index, (name, far, near) in enumerate(pairs):
        loads[name] = pltpu.make_async_copy(far, near, load.at[index])
        loads[name].start()

    def send(*args):
        copy = remote(*args)
        copy.start()
        started.append(copy)

    def wide(ref, first, last):
        return jnp.concatenate([ref[part, first:last, :] for part in range(parts)], axis=1)

    def arrived(ref, sem):
        remote(ref, ref, sem, sem, other).wait_recv()

    barrier = pltpu.get_barrier_semaphore()
    line = [{"graph": lax.rem(z + step, columns) * 2 + x} for step in range(1, columns)]
    for device in line + [beside, other]:
        pl.semaphore_signal(
            barrier, inc=1, device_id=device, device_id_type=pl.DeviceIdType.MESH
        )

    loads["emb"].wait()
    for group in range(groups):
        rows = []
        for c in range(4 * group, 4 * group + 4):
            if c < coeffs:
                rows.append(emb[:, c * width : (c + 1) * width].astype(jnp.float32))
            else:
                rows.append(jnp.zeros((atom_count, width), jnp.float32))
        x_all[me, 16 * group : 16 * group + 16, :] = jnp.concatenate(rows, axis=0).astype(jnp.bfloat16)
    own = x_all.at[me]
    pl.semaphore_wait(barrier, columns + 1)
    for step in range(1, columns):
        to = {"graph": lax.rem(z + step, columns) * 2 + x}
        send(own, own, y_send.at[step], y_recv.at[me], to)
    send(own, own, y_send.at[0], y_recv.at[me], beside)

    for name in ("w_rad", "dist", "live", "tgt", "rot", "cot", "owner", "local", "near_tgt"):
        loads[name].wait()
    pre = dot(dist[...], w_rad[...])
    sig = jax.nn.sigmoid(pre)
    alive = lax.broadcasted_iota(jnp.int32, (edges, width), 0) < live[0, 0]
    gate[...] = jnp.where(alive, pre * sig, 0.0)
    slope[...] = jnp.where(alive, sig + pre * sig * (1.0 - sig), 0.0)

    row = lax.broadcasted_iota(jnp.int32, (256, 256), 0)
    k, a = lax.rem(lax.div(row, 4), 4), lax.rem(row, 4)
    src_rows = 16 * peers
    fold = lax.div(lax.broadcasted_iota(jnp.int32, (256, 256), 1), edges)
    named = owner[...] * 4 + local[...]
    key_src = jnp.concatenate([named] * 4, axis=1) + fold * (4 * peers)
    key_tgt = jnp.concatenate([near_tgt[...]] * 4, axis=1) + fold * 4
    hit_src = (k * (4 * peers) + lax.div(row, 16) * 4 + a) == key_src
    hit_tgt = (k * 4 + a) == key_tgt
    hit = ((row < src_rows) & hit_src) | ((row >= src_rows) & (row < src_rows + 16) & hit_tgt)
    ones = jnp.where(hit, 1.0, 0.0)
    pick[...] = ones.astype(jnp.bfloat16)
    place[...] = ones.T.astype(jnp.bfloat16)

    rot_rows[...] = jnp.zeros_like(rot_rows)
    cot_rows[...] = jnp.zeros_like(cot_rows)
    for c in range(coeffs):
        block = rot[c].astype(jnp.float32)
        block = jnp.concatenate([block, jnp.zeros((deep - coeffs, edges), jnp.float32)], axis=0)
        rot_rows[c * edges : (c + 1) * edges, 0:deep] = block.T
        line = cot[:, c * width : (c + 1) * width].astype(jnp.float32)
        for part in range(parts):
            cot_rows[part, pl.ds(c, atom_count, stride=deep), :] = line[:, part * 128 : part * 128 + 128]
    cot_half[...] = wide(cot_rows, 0, atom_count * deep).reshape(cot_half.shape).astype(jnp.bfloat16)

    def edge(e, unused):
        r = rot_rows[pl.ds(e, tall, stride=edges), :][:, 0:deep].astype(jnp.bfloat16)
        turned = dot(r, cot_half[tgt[0, e]]).astype(jnp.bfloat16)
        back = dot(r, turned, FIRST)[0:tall]
        for part in range(parts):
            held[part, pl.ds(e, tall, stride=edges), :] = back[:, part * 128 : part * 128 + 128]
        return unused

    def forward(step):
        block = lax.rem(z - step + columns, columns) * 2 + x
        arrived(x_all.at[block], y_recv.at[block])
        send(x_all.at[block], x_all.at[block], f_send.at[step], y_recv.at[block], beside)

    for part in range(4):
        lax.fori_loop(part * (edges // 4), (part + 1) * (edges // 4), edge, 0, unroll=8)
        if 1 <= part < columns:
            forward(part)
    for step in range(4, columns):
        forward(step)

    for group in range(groups):
        rows = slice(group * 4 * edges, (group + 1) * 4 * edges)
        gated = wide(held, rows.start, rows.stop).reshape(4, edges, width) * gate[...][None]
        total = dot(pick[...], gated.reshape(4 * edges, width).astype(jnp.bfloat16))
        for p in range(peers):
            sums[p, 16 * group : 16 * group + 16, :] = total[16 * p : 16 * p + 16].astype(
                jnp.bfloat16
            )
        kept[16 * group : 16 * group + 16, :] = total[src_rows : src_rows + 16].astype(jnp.bfloat16)
    def across(step):
        goal = lax.rem(z + step, columns)
        send(sums.at[goal * 2 + 1 - x], from_x.at[goal], x_send.at[step], x_recv.at[goal], beside)

    early = max(1, columns - 2)
    for step in range(1, early + 1):
        across(step)

    half = width // 2
    cut, wider = half // peers, w_rad.shape[0] // 2 // peers
    split = cut + wider
    loads["w_src"].wait()
    loads["w_tgt"].wait()
    grad = dot(x_all[me], kept[...], FIRST).astype(jnp.bfloat16)
    share[:, :, 0:cut, :] = grad.reshape(2, peers, cut, width)
    y_tgt[...] = dot(x_all[me], w_tgt[...]).astype(jnp.bfloat16)

    for step in range(columns):
        block = step * 2 + 1 - x
        arrived(x_all.at[block], y_recv.at[block])
    for p in range(peers):
        y_all[p] = dot(x_all[p], w_src[...]).astype(jnp.bfloat16)
    gate_grad = jnp.zeros((edges, width), jnp.float32)
    spare = jnp.zeros((256 - src_rows - 16, width), jnp.bfloat16)
    for group in range(groups):
        near = [y_all[p, 16 * group : 16 * group + 16, :] for p in range(peers)]
        near = jnp.concatenate(near + [y_tgt[16 * group : 16 * group + 16, :], spare], axis=0)
        mixed = dot(place[...], near) * wide(
            held, group * 4 * edges, (group + 1) * 4 * edges
        )
        gate_grad = gate_grad + jnp.sum(mixed.reshape(4, edges, width), axis=0)
    pre_grad = (gate_grad * slope[...]).astype(jnp.bfloat16)
    grad = dot(dist[...], pre_grad, FIRST).astype(jnp.bfloat16)
    share[:, :, cut:split, :] = grad.reshape(2, peers, wider, width)
    tallest = peers * x_all.shape[1]
    grad = dot(x_all[...].reshape(tallest, width), sums[...].reshape(tallest, width), FIRST)
    share[:, :, split:, :] = grad.astype(jnp.bfloat16).reshape(2, peers, cut, width)
    send(share.at[1 - core], core_in, c_send.at[0], c_recv.at[0], other)

    arrived(core_in, c_recv.at[0])
    both[...] = (share[core].astype(jnp.float32) + core_in[...].astype(jnp.float32)).astype(
        jnp.bfloat16
    )
    for step in list(range(1, columns)) + [0]:
        goal = lax.rem(z + step, columns)
        send(both.at[goal * 2 + 1 - x], both_x.at[goal], d_send.at[step], d_recv.at[goal], beside)
    for step in list(range(early + 1, columns)) + [0]:
        across(step)

    def along(step):
        goal = lax.rem(z + step, columns)
        arrived(from_x.at[goal], x_recv.at[goal])
        to_z[goal] = (
            sums[goal * 2 + x].astype(jnp.float32) + from_x[goal].astype(jnp.float32)
        ).astype(jnp.bfloat16)
        send(to_z.at[goal], from_z.at[z], z_send.at[step], z_recv.at[z], {"graph": goal * 2 + x})

    for step in range(1, early + 1):
        along(step)

    for step in range(1, columns):
        goal = lax.rem(z + step, columns)
        arrived(both_x.at[goal], d_recv.at[goal])
        both_z[goal] = (
            both[goal * 2 + x].astype(jnp.float32) + both_x[goal].astype(jnp.float32)
        ).astype(jnp.bfloat16)
        to = {"graph": goal * 2 + x}
        send(both_z.at[goal], both_in.at[z], e_send.at[step], e_recv.at[z], to)
    arrived(both_x.at[z], d_recv.at[z])
    first = both[me].astype(jnp.float32) + both_x[z].astype(jnp.float32)
    for step in range(1, columns):
        origin = lax.rem(z + step, columns)
        arrived(both_in.at[origin], e_recv.at[origin])
        first = first + both_in[origin].astype(jnp.float32)
    whole[core, me] = first.astype(jnp.bfloat16)
    mine = whole.at[core, me]
    for step in range(1, columns):
        to = {"graph": lax.rem(z + step, columns) * 2 + x}
        send(mine, mine, g_send.at[step], g_recv.at[me], to)
    send(mine, mine, g_send.at[0], g_recv.at[me], beside)
    send(mine, mine, h_send.at[0], h_recv.at[me], other)

    for step in range(early + 1, columns):
        along(step)

    arrived(from_x.at[z], x_recv.at[z])
    total = sums[me].astype(jnp.float32) + from_x[z].astype(jnp.float32)
    for step in range(1, columns):
        origin = lax.rem(z + step, columns)
        arrived(from_z.at[origin], z_recv.at[origin])
        total = total + from_z[origin].astype(jnp.float32)
    total = total.astype(jnp.bfloat16)
    back = dot(total, w_src[...], LAST) + dot(kept[...], w_tgt[...], LAST)
    for c in range(coeffs):
        out_embed[:, c * width : (c + 1) * width] = back[4 * c : 4 * c + 4].astype(jnp.bfloat16)
    def spread(c, p):
        piece = whole[c, p].astype(jnp.float32) * scale
        at_tgt = pl.ds(pl.multiple_of(c * half + p * cut, cut), cut)
        at_rad = pl.ds(pl.multiple_of((c * peers + p) * wider, wider), wider)
        out_tgt[at_tgt, :] = piece[0:cut]
        out_rad[at_rad, :] = piece[cut:split]
        out_src[at_tgt, :] = piece[split:]

    spread(core, me)
    for step in range(1, columns):
        p = lax.rem(z + columns - step, columns) * 2 + x
        piece = whole.at[core, p]
        arrived(piece, g_recv.at[p])
        send(piece, piece, g_send.at[columns + step], g_recv.at[p], beside)
        send(piece, piece, h_send.at[step], h_recv.at[p], other)
        spread(core, p)
    for step in range(columns):
        p = lax.rem(z + columns - step, columns) * 2 + 1 - x
        piece = whole.at[core, p]
        arrived(piece, g_recv.at[p])
        send(piece, piece, h_send.at[columns + step], h_recv.at[p], other)
        spread(core, p)
    for step in range(peers):
        p = lax.rem(me + peers - step, peers)
        arrived(whole.at[1 - core, p], h_recv.at[p])
        spread(1 - core, p)
    for copy in started:
        copy.wait_send()


def near_shards(
    embed,
    cotangent,
    rotation,
    distance_feat,
    src_owner,
    src_local,
    tgt_local,
    live_count,
    w_src,
    w_tgt,
    w_radial,
):
    peers = lax.axis_size("graph")
    columns = peers // 2
    atom_count, row_len = embed.shape[1:]
    coeffs, edges = rotation.shape[1], rotation.shape[3]
    width, radial = w_src.shape[0], w_radial.shape[0]
    groups = -(-coeffs // 4)
    tall = -(-groups * 4 // 8) * 8
    deep = -(-tall // 16) * 16
    scale = 1.0 / math.sqrt(lax.axis_size("dp") * edges * peers * coeffs)
    cut = width // 2 // peers
    rows = 16 * groups
    bf16, f32 = jnp.bfloat16, jnp.float32
    split = cut + radial // 2 // peers
    vmem = pl.BlockSpec(memory_space=pltpu.VMEM)
    hbm = pl.BlockSpec(memory_space=pltpu.HBM)
    dma = pltpu.SemaphoreType.DMA
    i32 = jnp.int32
    scratch = [
        pltpu.VMEM(embed.shape[1:], bf16),
        pltpu.VMEM(cotangent.shape[1:], bf16),
        pltpu.VMEM(rotation.shape[1:], bf16),
        pltpu.VMEM(distance_feat.shape[1:], bf16),
        pltpu.VMEM((1, edges), i32),
        pltpu.VMEM((1, edges), i32),
        pltpu.VMEM((1, edges), i32),
        pltpu.SMEM((1, edges), i32),
        pltpu.SMEM((1, 1), i32),
        pltpu.VMEM(w_src.shape, bf16),
        pltpu.VMEM(w_tgt.shape, bf16),
        pltpu.VMEM(w_radial.shape, bf16),
        pltpu.VMEM((peers, rows, width), bf16),
        pltpu.VMEM((peers, rows, width), bf16),
        pltpu.VMEM((rows, width), bf16),
        pltpu.VMEM((tall * edges, 128), f32),
        pltpu.VMEM((width // 128, atom_count * deep, 128), f32),
        pltpu.VMEM((atom_count, deep, width), bf16),
        pltpu.VMEM((width // 128, tall * edges, 128), f32),
        pltpu.VMEM((edges, width), f32),
        pltpu.VMEM((edges, width), f32),
        pltpu.VMEM((256, 256), bf16),
        pltpu.VMEM((256, 256), bf16),
        pltpu.VMEM((peers, rows, width), bf16),
        pltpu.VMEM((rows, width), bf16),
        pltpu.VMEM((columns, rows, width), bf16),
        pltpu.VMEM((columns, rows, width), bf16),
        pltpu.VMEM((columns, rows, width), bf16),
        pltpu.VMEM((2, peers, split + cut, width), bf16),
        pltpu.VMEM((peers, split + cut, width), bf16),
        pltpu.VMEM((peers, split + cut, width), bf16),
        pltpu.VMEM((columns, split + cut, width), bf16),
        pltpu.VMEM((columns, split + cut, width), bf16),
        pltpu.VMEM((columns, split + cut, width), bf16),
        pltpu.VMEM((2, peers, split + cut, width), bf16),
    ]
    counts = [12, peers, peers] + [columns] * 5 + [1, 1] + [columns] * 4 + [peers] * 4
    grad_embed, grad_src, grad_tgt, grad_rad = pl.pallas_call(
        functools.partial(block_kernel, peers, scale),
        out_shape=(
            jax.ShapeDtypeStruct((atom_count, row_len), bf16),
            jax.ShapeDtypeStruct((width, width), f32),
            jax.ShapeDtypeStruct((width, width), f32),
            jax.ShapeDtypeStruct((radial, width), f32),
        ),
        in_specs=[hbm] * 11,
        out_specs=(vmem,) * 4,
        scratch_shapes=scratch + [dma((count,)) for count in counts],
        compiler_params=pltpu.CompilerParams(
            collective_id=0, has_side_effects=True, vmem_limit_bytes=63 * 1024 * 1024
        ),
    )(
        embed[0],
        cotangent[0],
        rotation[0],
        distance_feat[0],
        src_owner.reshape(1, edges),
        src_local,
        tgt_local,
        live_count,
        w_src,
        w_tgt,
        w_radial,
    )
    return grad_embed[None], grad_src, grad_tgt, grad_rad


def solution(mesh):
    peers = mesh.shape["graph"]
    near = peers in (4, 8) and mesh.shape["dp"] == 2
    placed = (
        P("dp", ("groups", "graph"), None),
        P("dp", ("groups", "graph"), None),
        P("dp", None, None, ("groups", "graph")),
        P("dp", ("groups", "graph"), None),
        P("dp", ("groups", "graph"), None),
        P("dp", ("groups", "graph")),
        P("dp", ("groups", "graph")),
        P("dp", ("groups", "graph")),
        P(),
        P(),
        P(),
    )
    return jax.shard_map(
        near_shards if near else shards,
        mesh=mesh,
        in_specs=placed,
        out_specs=(
            P("dp", ("groups", "graph"), None),
            P("groups", None),
            P("groups", None),
            P("groups", None),
        ),
        check_vma=False,
    )
```
